32 devices in a mesh: row: 4 (over z), col: 8 (over y, x, core).
Axes of the slice: x: 2, y: 2, z: 4, core: 2. Of those that a mesh axis runs over, the one named last changes fastest.
Arguments:
- momentum: float32 [8192, 28672], P('row', 'col'), may hold values from -400 to 400, as said below
- gradient: bfloat16 [8192, 28672], P('row', 'col'), may hold values from -3 to 3
- right_prev: float32 [28672, 256], P('col'), may hold values from -5 to 5
Outputs:
- new_momentum: float32 [8192, 28672], P('row', 'col')
- right_next: float32 [28672, 256], P('col')
- update: bfloat16 [8192, 28672], P('row', 'col')
The draws below stay inside these ranges and needn't reach their ends.
Inputs may be any that keep to these rules, and one draw needn't show every extreme that they name: momentum entries are finite reals.
All inputs are finite; a program needn't handle non-finite values.
Results may differ from the reference program's by a relative error of at most 0.001.
Values sent between devices are 32-bit elements; how exact they have to be, the bound alone decides.
A program may use at most 192 MiB of HBM per device.

```python
import math
import jax
import jax.numpy as jnp
from jax import lax

D = 8192
FF = 28672
RANK = 256


def draw_momentum(key, part):
    keys = jax.random.split(key, 3)
    rowpos = jnp.arange(D, dtype=jnp.float32)[:, None] / D
    colpos = jnp.arange(FF, dtype=jnp.float32)[None, :] / FF
    rise = 3.0
    values = jnp.clip(jax.random.normal(keys[0], (D, FF), jnp.float32), -5.0, 5.0)
    row_scale = jnp.exp(rowpos * math.log(rise) + jax.random.uniform(keys[1], (D, 1), jnp.float32, 0.0, math.log(3.2)))
    col_scale = jnp.exp(colpos * math.log(rise) + jax.random.uniform(keys[2], (1, FF), jnp.float32, 0.0, math.log(3.2)))
    return 0.3 * values * row_scale * col_scale


def level_of(stream_key, shape, cuts, least, largest):
    factor_of, own = 1.0, jax.random.fold_in(stream_key, 6)
    for axis_at, blocks in cuts:
        steps = jnp.exp(jax.random.uniform(jax.random.fold_in(own, axis_at), (blocks,), jnp.float32, least / len(cuts), largest / len(cuts)))
        factor_of = factor_of * jnp.repeat(steps, shape[axis_at] // blocks).reshape([-1 if axis == axis_at else 1 for axis in range(len(shape))])
    return factor_of


def bell_draw(rng, shape, width, limit, cuts=(), held_as=jnp.bfloat16):
    entries = width * jax.random.normal(rng, shape, jnp.float32)
    if cuts:
        entries = entries * level_of(rng, shape, cuts, -0.22, 0.18)
    return jnp.clip(entries, -limit, limit).astype(held_as)


def setup_inputs(seed: int = 0) -> dict:
    splits = jax.random.split(jax.random.key(seed), 4)
    return {
        "momentum": draw_momentum(jax.random.fold_in(splits[3], 71), 0),
        "gradient": bell_draw(splits[1], (D, FF), 0.5, 3.0, ((0, 4), (1, 8))),
        "right_prev": bell_draw(splits[2], (FF, RANK), 1.0, 5.0, ((0, 8),), jnp.float32),
    }


HI = lax.Precision.HIGHEST

def reference(momentum, gradient, right_prev):
    merged = momentum + gradient.astype(jnp.float32)
    left = jnp.dot(merged.astype(jnp.float32), right_prev.astype(jnp.float32), precision=HI, preferred_element_type=jnp.float32)
    gram = jnp.dot(left.T.astype(jnp.float32), left.astype(jnp.float32), precision=HI, preferred_element_type=jnp.float32)
    chol = jnp.linalg.cholesky(gram)
    ortho = jax.scipy.linalg.solve_triangular(chol, left.T, lower=True).T
    right = jnp.dot(merged.T.astype(jnp.float32), ortho.astype(jnp.float32), precision=HI, preferred_element_type=jnp.float32)
    colsq = lax.optimization_barrier(jnp.sum(right * right, axis=0))
    right_next = right * lax.rsqrt(colsq / FF + 1e-06)
    new_momentum = merged - 0.05 * jnp.dot(ortho.astype(jnp.float32), right.T.astype(jnp.float32), precision=HI, preferred_element_type=jnp.float32)
    factor = jnp.sqrt(jnp.float32(D) / jnp.float32(RANK))
    update = (factor * jnp.dot(ortho.astype(jnp.float32), right_next.T.astype(jnp.float32), precision=HI, preferred_element_type=jnp.float32)).astype(jnp.bfloat16)
    return (new_momentum, right_next, update)
```

```python
import functools
import jax
import jax.numpy as jnp
from jax import lax
from jax.experimental import pallas as pl
from jax.experimental.pallas import tpu as pltpu
from jax.sharding import PartitionSpec as P

HI = lax.Precision.HIGHEST
MESH = pl.DeviceIdType.MESH
F32, BF16 = jnp.float32, jnp.bfloat16
CHUNK = 128
PANEL = 16


def rcopy(src, dst, ssem, rsem, device):
    return pltpu.make_async_remote_copy(
        src_ref=src, dst_ref=dst, send_sem=ssem, recv_sem=rsem, device_id=device, device_id_type=MESH
    )


def signal(sem, device):
    pl.semaphore_signal(sem, inc=1, device_id=device, device_id_type=MESH)


def left_sum(chips, x_ref, o_ref, got, acc, sums, full, s1, r1, s2, r2, s3, r3, s4, r4):
    me = lax.axis_index("col")
    core, chip = lax.rem(me, 2), me // 2
    sib = {"col": me + 1 - 2 * core}
    barrier = pltpu.get_barrier_semaphore()
    signal(barrier, sib)
    for k in range(1, chips):
        signal(barrier, {"col": 2 * lax.rem(chip + k, chips) + core})
    pl.semaphore_wait(barrier, chips)

    def pair(k):
        q = lax.rem(chip + k, chips)
        return rcopy(x_ref.at[q, 1 - core], got.at[k], s1.at[k], r1.at[k], sib)

    def scatter(k):
        q = lax.rem(chip + k, chips)
        return rcopy(acc.at[k], sums.at[k - 1], s2.at[k - 1], r2.at[k - 1], {"col": 2 * q + core})

    order = list(range(chips // 2, chips)) + list(range(1, chips // 2)) + [0] if chips > 1 else [0]
    for k in order:
        pair(k).start()
    for k in order:
        pair(k).wait_recv()
        q = lax.rem(chip + k, chips)
        acc[k] = x_ref[q, core] + got[k]
        if k:
            scatter(k).start()
    total = acc[0]
    for k in [k for k in order if k]:
        scatter(k).wait_recv()
        total = total + sums[k - 1]
    full[chip, core] = total

    def gather(k):
        q = lax.rem(chip + k, chips)
        return rcopy(
            full.at[chip, core], full.at[chip, core], s3.at[k - 1], r3.at[k - 1], {"col": 2 * q + core}
        )

    def forward(k):
        q = lax.rem(chip - k + chips, chips)
        return rcopy(full.at[q, core], full.at[q, core], s4.at[k], r4.at[k], sib)

    for k in [k for k in order if k]:
        gather(k).start()
    forward(0).start()
    for k in [k for k in order if k]:
        q = lax.rem(chip - k + chips, chips)
        rcopy(
            full.at[q, core], full.at[q, core], s3.at[k - 1], r3.at[k - 1], {"col": 2 * q + core}
        ).wait_recv()
        forward(k).start()
    for k in range(chips):
        q = lax.rem(chip - k + chips, chips)
        rcopy(full.at[q, 1 - core], full.at[q, 1 - core], s4.at[k], r4.at[k], sib).wait_recv()
    for k in range(chips):
        pair(k).wait_send()
        forward(k).wait_send()
        if k:
            scatter(k).wait_send()
            gather(k).wait_send()
    o_ref[...] = full[...]


def all_reduce_left(part, n):
    rows, rank = part.shape
    chips, s = n // 2, rows // n
    dma = pltpu.SemaphoreType.DMA
    out = pl.pallas_call(
        functools.partial(left_sum, chips),
        out_shape=jax.ShapeDtypeStruct((chips, 2, s, rank), F32),
        in_specs=[pl.BlockSpec(memory_space=pltpu.VMEM)],
        out_specs=pl.BlockSpec(memory_space=pltpu.VMEM),
        scratch_shapes=[
            pltpu.VMEM((chips, s, rank), F32),
            pltpu.VMEM((chips, s, rank), F32),
            pltpu.VMEM((max(chips - 1, 1), s, rank), F32),
            pltpu.VMEM((chips, 2, s, rank), F32),
            dma((chips,)), dma((chips,)),
            dma((max(chips - 1, 1),)), dma((max(chips - 1, 1),)),
            dma((max(chips - 1, 1),)), dma((max(chips - 1, 1),)),
            dma((chips,)), dma((chips,)),
        ],
        compiler_params=pltpu.CompilerParams(
            collective_id=0, has_side_effects=True, vmem_limit_bytes=32 * 2**20
        ),
        name="left_sum",
    )(part.reshape(chips, 2, s, rank))
    return out.reshape(rows, rank)


def panel_step(mat, p):
    rank, wide = mat.shape
    first = p * PANEL
    rows0 = pl.ds(pl.multiple_of(first, PANEL), PANEL)
    sub = lax.broadcasted_iota(jnp.int32, (PANEL, wide), 0)
    lane = lax.broadcasted_iota(jnp.int32, (PANEL, wide), 1)

    def step(k, block):
        col = jnp.sum(jnp.where(lane == first + k, block, 0.0), axis=1, keepdims=True)
        row = jnp.sum(jnp.where(sub == k, block, 0.0), axis=0, keepdims=True)
        pivot = jnp.sum(jnp.where(sub[:, :1] == k, col, 0.0), axis=0, keepdims=True)
        inv = lax.rsqrt(pivot)
        inv = inv * (1.5 - 0.5 * (pivot * inv) * inv)
        u = row * inv
        factor = jnp.where(sub[:, :1] > k, col * inv, 0.0)
        return jnp.where(sub == k, u, block - factor * u)

    u = lax.fori_loop(0, PANEL, step, mat[rows0, :])
    mat[rows0, :] = u
    drop = lax.dot_general(
        u[:, :rank], u, (((0,), (0,)), ((), ())), precision=HI, preferred_element_type=F32
    )
    below = lax.broadcasted_iota(jnp.int32, (rank, wide), 0) >= first + PANEL
    mat[...] = jnp.where(below, mat[...] - drop, mat[...])


def times_inverse(a, inverse):
    return lax.dot_general(
        a, inverse, (((1,), (1,)), ((), ())), precision=HI, preferred_element_type=F32
    )


def split(a):
    hi = a.astype(BF16)
    return hi, (a - hi.astype(F32)).astype(BF16)


def right_sum(
    n, cols, ff, gram_ref, w_ref, left_ref,
    next_ref, nh_ref, nl_ref, rb_ref, oh_ref, ol_ref,
    x, outer_in, inner_in, mat, colsq, s_in, r_outer, s_out, r_inner, s_c, r_c,
):
    me, mc = lax.axis_index("row"), lax.axis_index("col")
    half = n // 2
    low = me < half
    depth = jnp.where(low, half - 1 - me, me - half)
    inward = {"row": jnp.where(low, me + 1, me - 1)}
    has_outer = depth < half - 1
    outward = {"row": jnp.where(has_outer, jnp.where(low, me - 1, me + 1), me)}
    rank = gram_ref.shape[0]
    ffl = w_ref.shape[0]
    chunks = (rank + ffl) // CHUNK
    gram_chunks, panels = rank // CHUNK, rank // PANEL

    barrier = pltpu.get_barrier_semaphore()
    for k in range(1, cols):
        signal(barrier, {"col": lax.rem(mc + k, cols)})
    signal(barrier, inward)

    @pl.when(has_outer)
    def _():
        signal(barrier, outward)

    @pl.when(has_outer)
    def _():
        pl.semaphore_wait(barrier, cols + 1)

    @pl.when(jnp.logical_not(has_outer))
    def _():
        pl.semaphore_wait(barrier, cols)

    x[pl.ds(0, rank), :] = gram_ref[...]
    x[pl.ds(rank, ffl), :] = w_ref[...]

    def at(c):
        return pl.ds(pl.multiple_of(c * CHUNK, CHUNK), CHUNK)

    def to_inner(c):
        return rcopy(x.at[at(c)], outer_in.at[at(c)], s_in.at[c], r_outer.at[c], inward)

    def to_partner(c):
        return rcopy(x.at[at(c)], inner_in.at[at(c)], s_in.at[c], r_inner.at[c], inward)

    def to_outer(c):
        return rcopy(outer_in.at[at(c)], inner_in.at[at(c)], s_out.at[c], r_inner.at[c], outward)

    lag = 2 + 3 * depth

    def turn(t, carry):
        @pl.when(t < chunks)
        def _():
            @pl.when(has_outer)
            def _():
                to_inner(t).wait_recv()
                x[at(t), :] = x[at(t), :] + outer_in[at(t), :]

            @pl.when(depth > 0)
            def _():
                to_inner(t).start()

            @pl.when(depth == 0)
            def _():
                to_partner(t).start()

        c = t - lag

        @pl.when((c >= 0) & (c < chunks))
        def _():
            to_partner(c).wait_recv()

            @pl.when(depth == 0)
            def _():
                outer_in[at(c), :] = x[at(c), :] + inner_in[at(c), :]

            @pl.when(depth > 0)
            def _():
                outer_in[at(c), :] = inner_in[at(c), :]

            @pl.when(has_outer)
            def _():
                to_outer(c).start()

        @pl.when(c == gram_chunks - 1)
        def _():
            mat[:, pl.ds(0, rank)] = outer_in[pl.ds(0, rank), :]
            i0 = lax.broadcasted_iota(jnp.int32, (rank, rank), 0)
            i1 = lax.broadcasted_iota(jnp.int32, (rank, rank), 1)
            mat[:, pl.ds(rank, rank)] = jnp.where(i0 == i1, 1.0, 0.0).astype(F32)

        @pl.when((c >= gram_chunks) & (c < gram_chunks + panels))
        def _():
            panel_step(mat, c - gram_chunks)

        return carry

    turns = max(chunks, gram_chunks + panels) + 2 + 3 * (half - 1)
    lax.fori_loop(0, turns, turn, 0)

    inverse = mat[:, pl.ds(rank, rank)]

    def to_right(b, total):
        here = pl.ds(pl.multiple_of(b * CHUNK, CHUNK), CHUNK)
        there = pl.ds(pl.multiple_of(rank + b * CHUNK, CHUNK), CHUNK)
        value = times_inverse(outer_in[there, :], inverse)
        next_ref[here, :] = value
        rb_ref[here, :] = (0.05 * value).astype(BF16)
        return total + jnp.sum(value * value, axis=0, keepdims=True)

    part = lax.fori_loop(0, ffl // CHUNK, to_right, jnp.zeros((1, rank), F32))
    colsq[mc] = jnp.broadcast_to(part, (8, rank))

    def share(k):
        return rcopy(
            colsq.at[mc], colsq.at[mc], s_c.at[k - 1], r_c.at[k - 1], {"col": lax.rem(mc + k, cols)}
        )

    for k in range(1, cols):
        share(k).start()

    def to_ortho(b, carry):
        here = pl.ds(pl.multiple_of(b * CHUNK, CHUNK), CHUNK)
        hi, lo = split(times_inverse(left_ref[here, :], inverse))
        oh_ref[here, :] = hi
        ol_ref[here, :] = lo
        return carry

    lax.fori_loop(0, left_ref.shape[0] // CHUNK, to_ortho, 0)

    for k in range(1, cols):
        q = lax.rem(mc - k + cols, cols)
        rcopy(colsq.at[q], colsq.at[q], s_c.at[k - 1], r_c.at[k - 1], {"col": q}).wait_recv()
    total = colsq[0]
    for q in range(1, cols):
        total = total + colsq[q]
    scale = 1.0 / jnp.sqrt(total[:1] / ff + 1e-6)

    def to_next(b, carry):
        here = pl.ds(pl.multiple_of(b * CHUNK, CHUNK), CHUNK)
        value = next_ref[here, :] * scale
        next_ref[here, :] = value
        hi, lo = split(value)
        nh_ref[here, :] = hi
        nl_ref[here, :] = lo
        return carry

    lax.fori_loop(0, ffl // CHUNK, to_next, 0)

    def drain(c, carry):
        to_inner(c).wait_send()

        @pl.when(has_outer)
        def _():
            to_outer(c).wait_send()

        return carry

    lax.fori_loop(0, chunks, drain, 0)
    for k in range(1, cols):
        share(k).wait_send()


def right_factor(gram, w, left, n, cols, ff):
    rank, ffl, rows = gram.shape[0], w.shape[0], left.shape[0]
    chunks = (rank + ffl) // CHUNK
    dma = pltpu.SemaphoreType.DMA
    vm = pl.BlockSpec(memory_space=pltpu.VMEM)
    return pl.pallas_call(
        functools.partial(right_sum, n, cols, float(ff)),
        out_shape=[
            jax.ShapeDtypeStruct((ffl, rank), F32),
            jax.ShapeDtypeStruct((ffl, rank), BF16),
            jax.ShapeDtypeStruct((ffl, rank), BF16),
            jax.ShapeDtypeStruct((ffl, rank), BF16),
            jax.ShapeDtypeStruct((rows, rank), BF16),
            jax.ShapeDtypeStruct((rows, rank), BF16),
        ],
        in_specs=[vm] * 3,
        out_specs=[vm] * 6,
        scratch_shapes=[
            pltpu.VMEM((rank + ffl, rank), F32),
            pltpu.VMEM((rank + ffl, rank), F32),
            pltpu.VMEM((rank + ffl, rank), F32),
            pltpu.VMEM((rank, 2 * rank), F32),
            pltpu.VMEM((cols, 8, rank), F32),
            dma((chunks,)), dma((chunks,)), dma((chunks,)), dma((chunks,)),
            dma((cols - 1,)), dma((cols - 1,)),
        ],
        compiler_params=pltpu.CompilerParams(
            collective_id=1, has_side_effects=True, vmem_limit_bytes=48 * 2**20
        ),
        name="right_sum",
    )(gram, w, left)


def finish(factor, m_ref, g_ref, oh_ref, ol_ref, nh_ref, nl_ref, rb_ref, new_ref, up_ref):
    def nt(a, b):
        return lax.dot_general(a, b, (((1,), (1,)), ((), ())), preferred_element_type=F32)

    oh = oh_ref[...]
    new_ref[...] = (m_ref[...] + g_ref[...].astype(F32)) - nt(oh, rb_ref[...])
    up = nt(oh, nh_ref[...]) + (nt(oh, nl_ref[...]) + nt(ol_ref[...], nh_ref[...]))
    up_ref[...] = (factor * up).astype(BF16)


def divisor(size, most):
    return max(t for t in range(128, most + 1, 128) if size % t == 0)


def outputs(m, g, oh, ol, nh, nl, rb, factor):
    rows, cols = m.shape
    rank = oh.shape[1]
    tm, tn = divisor(rows, 256), divisor(cols, 1792)
    tile = pl.BlockSpec((tm, tn), lambda j, i: (i, j))
    o = pl.BlockSpec((tm, rank), lambda j, i: (i, 0))
    r = pl.BlockSpec((tn, rank), lambda j, i: (j, 0))
    return pl.pallas_call(
        functools.partial(finish, factor),
        grid=(cols // tn, rows // tm),
        out_shape=[jax.ShapeDtypeStruct((rows, cols), F32), jax.ShapeDtypeStruct((rows, cols), BF16)],
        in_specs=[tile, tile, o, o, r, r, r],
        out_specs=[tile, tile],
        compiler_params=pltpu.CompilerParams(vmem_limit_bytes=48 * 2**20),
        name="finish",
    )(m, g, oh, ol, nh, nl, rb)


def solution(mesh):
    n, cols = mesh.shape["row"], mesh.shape["col"]

    def on_device(momentum, gradient, right_prev):
        ff, rank = right_prev.shape[0] * cols, right_prev.shape[1]
        d = momentum.shape[0] * n
        merged = momentum + gradient.astype(F32)
        part = jnp.dot(merged, right_prev, precision=lax.Precision.HIGH, preferred_element_type=F32)
        left = all_reduce_left(part, cols)
        gram = jnp.dot(left.T, left, precision=HI, preferred_element_type=F32)
        w = jnp.dot(merged.T, left, precision=lax.Precision.HIGH, preferred_element_type=F32)
        right_next, nh, nl, rb, oh, ol = right_factor(gram, w, left, n, cols, ff)
        new_momentum, update = outputs(
            momentum, gradient, oh, ol, nh, nl, rb, (d / rank) ** 0.5
        )
        return new_momentum, right_next, update

    in_specs = (P("row", "col"), P("row", "col"), P("col", None))
    out_specs = (P("row", "col"), P("col", None), P("row", "col"))
    return jax.shard_map(
        on_device, mesh=mesh, in_specs=in_specs, out_specs=out_specs, check_vma=False
    )
```

```python
import functools
import jax
import jax.numpy as jnp
from jax import lax
from jax.experimental import pallas as pl
from jax.experimental.pallas import tpu as pltpu
from jax.sharding import PartitionSpec as P

HI = lax.Precision.HIGHEST
MESH = pl.DeviceIdType.MESH
F32, BF16 = jnp.float32, jnp.bfloat16
CHUNK = 128
PANEL = 16


def rcopy(src, dst, ssem, rsem, device):
    return pltpu.make_async_remote_copy(
        src_ref=src, dst_ref=dst, send_sem=ssem, recv_sem=rsem, device_id=device, device_id_type=MESH
    )


def signal(sem, device):
    pl.semaphore_signal(sem, inc=1, device_id=device, device_id_type=MESH)


def split(a):
    hi = a.astype(BF16)
    return hi, (a - hi.astype(F32)).astype(BF16)


def dot(a, b):
    return jnp.dot(a, b, preferred_element_type=F32)


def dot3(ah, al, bh, bl):
    return dot(ah, bh) + (dot(ah, bl) + dot(al, bh))


def left_sum(chips, fused, *refs):
    if fused:
        m_ref, g_ref, rp_ref, o_ref, x, rh, rl, mbuf, gbuf, sf, *refs = refs
    else:
        x, o_ref, *refs = refs
    got, acc, sums, full, s1, r1, s2, r2, s3, r3, s4, r4 = refs
    me = lax.axis_index("col")
    core, chip = lax.rem(me, 2), me // 2
    sib = {"col": me + 1 - 2 * core}
    s = acc.shape[1]

    def place(i):
        k = lax.rem(lax.rem(i, chips) + 1, chips)
        return k, lax.rem(chip + k, chips), jnp.where(i < chips, 1 - core, core)

    def fetch(i):
        _, q, c = place(i)
        rows = pl.ds(pl.multiple_of((2 * q + c) * s, s), s)
        slot = lax.rem(i, 2)
        return (
            pltpu.make_async_copy(m_ref.at[rows], mbuf.at[slot], sf.at[0, slot]),
            pltpu.make_async_copy(g_ref.at[rows], gbuf.at[slot], sf.at[1, slot]),
        )

    if fused:
        for f in fetch(0):
            f.start()
    barrier = pltpu.get_barrier_semaphore()
    signal(barrier, sib)
    for k in range(1, chips):
        signal(barrier, {"col": 2 * lax.rem(chip + k, chips) + core})
    if fused:
        hi, lo = split(rp_ref[...])
        rh[...] = hi
        rl[...] = lo
    pl.semaphore_wait(barrier, chips)

    def pair(k):
        q = lax.rem(chip + k, chips)
        return rcopy(x.at[q, 1 - core], got.at[k], s1.at[k], r1.at[k], sib)

    def scatter(k):
        q = lax.rem(chip + k, chips)
        return rcopy(acc.at[k], sums.at[k], s2.at[k], r2.at[k], {"col": 2 * q + core})

    def turn(i, carry):
        k, q, c = place(i)
        if fused:
            @pl.when(i + 1 < 2 * chips)
            def _():
                for f in fetch(i + 1):
                    f.start()

            for f in fetch(i):
                f.wait()
            slot = lax.rem(i, 2)
            depth = rh.shape[0]
            step = divisor(depth, 512)
            total = jnp.zeros((s, rh.shape[1]), F32)
            for at in range(0, depth, step):
                here = pl.ds(at, step)
                hi, lo = split(mbuf[slot, :, here] + gbuf[slot, :, here].astype(F32))
                total = total + dot3(hi, lo, rh[here, :], rl[here, :])
            x[q, c] = total

        @pl.when(i < chips)
        def _():
            pair(k).start()

        @pl.when(i >= chips)
        def _():
            pair(k).wait_recv()
            acc[k] = x[q, core] + got[k]

            @pl.when(k > 0)
            def _():
                scatter(k).start()

        return carry

    lax.fori_loop(0, 2 * chips, turn, 0)
    total = acc[0]
    for k in range(1, chips):
        scatter(k).wait_recv()
        total = total + sums[k]
    full[chip, core] = total

    def gather(k):
        q = lax.rem(chip + k, chips)
        return rcopy(full.at[chip, core], full.at[chip, core], s3.at[k], r3.at[k], {"col": 2 * q + core})

    def forward(k):
        q = lax.rem(chip - k + chips, chips)
        return rcopy(full.at[q, core], full.at[q, core], s4.at[k], r4.at[k], sib)

    for k in range(1, chips):
        gather(k).start()
    forward(0).start()
    for k in range(1, chips):
        q = lax.rem(chip - k + chips, chips)
        rcopy(full.at[q, core], full.at[q, core], s3.at[k], r3.at[k], {"col": 2 * q + core}).wait_recv()
        forward(k).start()
    for k in range(chips):
        q = lax.rem(chip - k + chips, chips)
        rcopy(full.at[q, 1 - core], full.at[q, 1 - core], s4.at[k], r4.at[k], sib).wait_recv()
    for k in range(chips):
        pair(k).wait_send()
        forward(k).wait_send()
        if k:
            scatter(k).wait_send()
            gather(k).wait_send()
    o_ref[...] = full[...]


def left_factor(momentum, gradient, right_prev, n):
    rows, ffl = momentum.shape
    rank = right_prev.shape[1]
    chips, s = n // 2, rows // n
    fused = s % 16 == 0
    dma = pltpu.SemaphoreType.DMA
    vm = pl.BlockSpec(memory_space=pltpu.VMEM)
    hbm = pl.BlockSpec(memory_space=pl.ANY)
    if fused:
        args, specs = (momentum, gradient, right_prev), [hbm, hbm, vm]
        extra = [
            pltpu.VMEM((chips, 2, s, rank), F32),
            pltpu.VMEM((ffl, rank), BF16),
            pltpu.VMEM((ffl, rank), BF16),
            pltpu.VMEM((2, s, ffl), F32),
            pltpu.VMEM((2, s, ffl), BF16),
            dma((2, 2)),
        ]
    else:
        merged = momentum + gradient.astype(F32)
        part = jnp.dot(merged, right_prev, precision=lax.Precision.HIGH, preferred_element_type=F32)
        args, specs, extra = (part.reshape(chips, 2, s, rank),), [vm], []
    out = pl.pallas_call(
        functools.partial(left_sum, chips, fused),
        out_shape=jax.ShapeDtypeStruct((chips, 2, s, rank), F32),
        in_specs=specs,
        out_specs=vm,
        scratch_shapes=extra
        + [pltpu.VMEM((chips, s, rank), F32)] * 3
        + [pltpu.VMEM((chips, 2, s, rank), F32)]
        + [dma((chips,))] * 8,
        compiler_params=pltpu.CompilerParams(
            collective_id=0, has_side_effects=True, vmem_limit_bytes=48 * 2**20
        ),
        name="left_sum",
    )(*args)
    return out.reshape(rows, rank)


def panel_step(mat, p):
    rank, wide = mat.shape
    first = p * PANEL
    rows0 = pl.ds(pl.multiple_of(first, PANEL), PANEL)
    rows = mat[rows0, :]
    pick = lax.broadcasted_iota(jnp.int32, (rank, 128), 0) == first + lax.broadcasted_iota(
        jnp.int32, (rank, 128), 1
    )
    block = jnp.dot(rows[:, :rank], pick.astype(F32), precision=HI, preferred_element_type=F32)
    sub = lax.broadcasted_iota(jnp.int32, (PANEL, 128), 0)
    lane = lax.broadcasted_iota(jnp.int32, (PANEL, 128), 1)
    block = jnp.where(lane < PANEL, block, jnp.where(lane - PANEL == sub, 1.0, 0.0))
    for k in range(PANEL):
        col = jnp.broadcast_to(block[:, k : k + 1], (PANEL, 128))
        pivot = jnp.broadcast_to(col[k : k + 1, :], (PANEL, 128))
        inv = lax.rsqrt(pivot)
        inv = inv * (1.5 - 0.5 * (pivot * inv) * inv)
        u = jnp.broadcast_to(block[k : k + 1, :], (PANEL, 128)) * inv
        factor = jnp.where(sub > k, col * inv, 0.0)
        block = jnp.where(sub == k, u, block - factor * u)
    u = jnp.dot(block[:, PANEL : 2 * PANEL], rows, precision=HI, preferred_element_type=F32)
    mat[rows0, :] = u
    drop = lax.dot_general(
        u[:, :rank], u, (((0,), (0,)), ((), ())), precision=HI, preferred_element_type=F32
    )
    below = lax.broadcasted_iota(jnp.int32, (rank, wide), 0) >= first + PANEL
    mat[...] = jnp.where(below, mat[...] - drop, mat[...])


def times_inverse(a, inverse):
    return lax.dot_general(
        a, inverse, (((1,), (1,)), ((), ())), precision=HI, preferred_element_type=F32
    )


def right_sum(
    n, cols, ff, m_ref, g_ref, left_ref,
    next_ref, nh_ref, nl_ref, rb_ref, oh_ref, ol_ref,
    x, outer_in, inner_in, mat, colsq, lh, ll, mbuf, gbuf, sf, s_in, r_outer, s_out, r_inner, s_c, r_c,
):
    me, mc = lax.axis_index("row"), lax.axis_index("col")
    half = n // 2
    low = me < half
    depth = jnp.where(low, half - 1 - me, me - half)
    inward = {"row": jnp.where(low, me + 1, me - 1)}
    has_outer = depth < half - 1
    outward = {"row": jnp.where(has_outer, jnp.where(low, me - 1, me + 1), me)}
    rows, rank = left_ref.shape
    ffl = m_ref.shape[1]
    chunks = (rank + ffl) // CHUNK
    gram_chunks, panels = rank // CHUNK, rank // PANEL
    spread = max(chunks - gram_chunks, panels)

    def fetch(w):
        here = pl.ds(pl.multiple_of(w * CHUNK, CHUNK), CHUNK)
        slot = lax.rem(w, 2)
        return (
            pltpu.make_async_copy(m_ref.at[:, here], mbuf.at[slot], sf.at[0, slot]),
            pltpu.make_async_copy(g_ref.at[:, here], gbuf.at[slot], sf.at[1, slot]),
        )

    for f in fetch(0):
        f.start()

    barrier = pltpu.get_barrier_semaphore()
    for k in range(1, cols):
        signal(barrier, {"col": lax.rem(mc + k, cols)})
    signal(barrier, inward)

    @pl.when(has_outer)
    def _():
        signal(barrier, outward)

    for b in range(0, rows, CHUNK):
        hi, lo = split(left_ref[pl.ds(b, CHUNK), :].T)
        lh[:, pl.ds(b, CHUNK)] = hi
        ll[:, pl.ds(b, CHUNK)] = lo
    gram = lax.dot_general(
        left_ref[...], left_ref[...], (((0,), (0,)), ((), ())), precision=HI, preferred_element_type=F32
    )
    for c in range(gram_chunks):
        x[c] = gram[:, c * CHUNK : (c + 1) * CHUNK]

    @pl.when(has_outer)
    def _():
        pl.semaphore_wait(barrier, cols + 1)

    @pl.when(jnp.logical_not(has_outer))
    def _():
        pl.semaphore_wait(barrier, cols)

    def to_inner(c):
        return rcopy(x.at[c], outer_in.at[c], s_in.at[c], r_outer.at[c], inward)

    def to_partner(c):
        return rcopy(x.at[c], inner_in.at[c], s_in.at[c], r_inner.at[c], inward)

    def to_outer(c):
        return rcopy(outer_in.at[c], inner_in.at[c], s_out.at[c], r_inner.at[c], outward)

    lag = 2 + 3 * depth

    def turn(t, carry):
        @pl.when((t >= gram_chunks) & (t < chunks))
        def _():
            w = t - gram_chunks

            @pl.when(w + 1 < chunks - gram_chunks)
            def _():
                for f in fetch(w + 1):
                    f.start()

            for f in fetch(w):
                f.wait()
            slot = lax.rem(w, 2)
            step = divisor(rows, 512)
            total = jnp.zeros((rank, CHUNK), F32)
            for b in range(0, rows, step):
                here = pl.ds(b, step)
                hi, lo = split(mbuf[slot, here, :] + gbuf[slot, here, :].astype(F32))
                total = total + dot3(lh[:, here], ll[:, here], hi, lo)
            x[t] = total

        @pl.when(t < chunks)
        def _():
            @pl.when(has_outer)
            def _():
                to_inner(t).wait_recv()
                x[t] = x[t] + outer_in[t]

            @pl.when(depth > 0)
            def _():
                to_inner(t).start()

            @pl.when(depth == 0)
            def _():
                to_partner(t).start()

        c = t - lag

        @pl.when((c >= 0) & (c < chunks))
        def _():
            to_partner(c).wait_recv()

            @pl.when(depth == 0)
            def _():
                outer_in[c] = x[c] + inner_in[c]

            @pl.when(depth > 0)
            def _():
                outer_in[c] = inner_in[c]

            @pl.when(has_outer)
            def _():
                to_outer(c).start()

        @pl.when(c == gram_chunks - 1)
        def _():
            for b in range(gram_chunks):
                mat[:, pl.ds(b * CHUNK, CHUNK)] = outer_in[b]
            i0 = lax.broadcasted_iota(jnp.int32, (rank, rank), 0)
            i1 = lax.broadcasted_iota(jnp.int32, (rank, rank), 1)
            mat[:, pl.ds(rank, rank)] = jnp.where(i0 == i1, 1.0, 0.0).astype(F32)

        at = jnp.maximum(c - gram_chunks, 0)
        p = at * panels // spread

        @pl.when((c >= gram_chunks) & (c < gram_chunks + spread) & ((at + 1) * panels // spread > p))
        def _():
            panel_step(mat, p)

        return carry

    turns = gram_chunks + spread + 2 + 3 * (half - 1)
    lax.fori_loop(0, turns, turn, 0)

    inverse = mat[:, pl.ds(rank, rank)]

    def to_right(b, total):
        here = pl.ds(pl.multiple_of(b * CHUNK, CHUNK), CHUNK)
        c = b + gram_chunks
        value = jnp.dot(inverse, outer_in[c], precision=HI, preferred_element_type=F32)
        inner_in[c] = value
        rb_ref[:, here] = (0.05 * value).astype(BF16)
        return total + value * value

    part = lax.fori_loop(0, ffl // CHUNK, to_right, jnp.zeros((rank, CHUNK), F32))
    colsq[mc] = jnp.broadcast_to(jnp.sum(part.T, axis=0, keepdims=True), (8, rank))

    def share(k):
        return rcopy(
            colsq.at[mc], colsq.at[mc], s_c.at[k - 1], r_c.at[k - 1], {"col": lax.rem(mc + k, cols)}
        )

    for k in range(1, cols):
        share(k).start()

    def to_ortho(b, carry):
        here = pl.ds(pl.multiple_of(b * CHUNK, CHUNK), CHUNK)
        hi, lo = split(times_inverse(left_ref[here, :], inverse))
        oh_ref[here, :] = hi
        ol_ref[here, :] = lo
        return carry

    lax.fori_loop(0, left_ref.shape[0] // CHUNK, to_ortho, 0)

    for k in range(1, cols):
        q = lax.rem(mc - k + cols, cols)
        rcopy(colsq.at[q], colsq.at[q], s_c.at[k - 1], r_c.at[k - 1], {"col": q}).wait_recv()
    total = colsq[0]
    for q in range(1, cols):
        total = total + colsq[q]
    scale = jnp.broadcast_to(1.0 / jnp.sqrt(total[:1] / ff + 1e-6), (CHUNK, rank)).T

    def to_next(b, carry):
        here = pl.ds(pl.multiple_of(b * CHUNK, CHUNK), CHUNK)
        value = inner_in[b + gram_chunks] * scale
        next_ref[here, :] = value.T
        hi, lo = split(value)
        nh_ref[:, here] = hi
        nl_ref[:, here] = lo
        return carry

    lax.fori_loop(0, ffl // CHUNK, to_next, 0)

    def drain(c, carry):
        to_inner(c).wait_send()

        @pl.when(has_outer)
        def _():
            to_outer(c).wait_send()

        return carry

    lax.fori_loop(0, chunks, drain, 0)
    for k in range(1, cols):
        share(k).wait_send()


def right_factor(momentum, gradient, left, n, cols, ff):
    (rows, rank), ffl = left.shape, momentum.shape[1]
    chunks = (rank + ffl) // CHUNK
    dma = pltpu.SemaphoreType.DMA
    vm = pl.BlockSpec(memory_space=pltpu.VMEM)
    hbm = pl.BlockSpec(memory_space=pl.ANY)
    return pl.pallas_call(
        functools.partial(right_sum, n, cols, float(ff)),
        out_shape=[jax.ShapeDtypeStruct((ffl, rank), F32)]
        + [jax.ShapeDtypeStruct((rank, ffl), BF16)] * 3
        + [jax.ShapeDtypeStruct((rows, rank), BF16)] * 2,
        in_specs=[hbm, hbm, vm],
        out_specs=[vm] * 6,
        scratch_shapes=[pltpu.VMEM((chunks, rank, CHUNK), F32)] * 3
        + [
            pltpu.VMEM((rank, 2 * rank), F32),
            pltpu.VMEM((cols, 8, rank), F32),
            pltpu.VMEM((rank, rows), BF16),
            pltpu.VMEM((rank, rows), BF16),
            pltpu.VMEM((2, rows, CHUNK), F32),
            pltpu.VMEM((2, rows, CHUNK), BF16),
            dma((2, 2)),
        ]
        + [dma((chunks,))] * 4
        + [dma((cols - 1,))] * 2,
        compiler_params=pltpu.CompilerParams(
            collective_id=1, has_side_effects=True, vmem_limit_bytes=48 * 2**20
        ),
        name="right_sum",
    )(momentum, gradient, left)


def finish(factor, m_ref, g_ref, oh_ref, ol_ref, nh_ref, nl_ref, rb_ref, new_ref, up_ref):
    oh, nh = oh_ref[...], nh_ref[...]
    new_ref[...] = (m_ref[...] + g_ref[...].astype(F32)) - dot(oh, rb_ref[...])
    up = dot(
        jnp.concatenate([oh, oh, ol_ref[...]], axis=1), jnp.concatenate([nh, nl_ref[...], nh], axis=0)
    )
    up_ref[...] = (factor * up).astype(BF16)


def divisor(size, most):
    return max(t for t in range(128, most + 1, 128) if size % t == 0)


def outputs(m, g, oh, ol, nh, nl, rb, factor):
    rows, cols = m.shape
    rank = oh.shape[1]
    tm, tn = divisor(rows, 256), divisor(cols, 1792)
    tile = pl.BlockSpec((tm, tn), lambda j, i: (i, j))
    o = pl.BlockSpec((tm, rank), lambda j, i: (i, 0))
    r = pl.BlockSpec((rank, tn), lambda j, i: (0, j))
    return pl.pallas_call(
        functools.partial(finish, factor),
        grid=(cols // tn, rows // tm),
        out_shape=[jax.ShapeDtypeStruct((rows, cols), F32), jax.ShapeDtypeStruct((rows, cols), BF16)],
        in_specs=[tile, tile, o, o, r, r, r],
        out_specs=[tile, tile],
        compiler_params=pltpu.CompilerParams(vmem_limit_bytes=48 * 2**20),
        name="finish",
    )(m, g, oh, ol, nh, nl, rb)


def solution(mesh):
    n, cols = mesh.shape["row"], mesh.shape["col"]

    def on_device(momentum, gradient, right_prev):
        ff, rank = right_prev.shape[0] * cols, right_prev.shape[1]
        d = momentum.shape[0] * n
        left = left_factor(momentum, gradient, right_prev, cols)
        right_next, nh, nl, rb, oh, ol = right_factor(momentum, gradient, left, n, cols, ff)
        new_momentum, update = outputs(
            momentum, gradient, oh, ol, nh, nl, rb, (d / rank) ** 0.5
        )
        return new_momentum, right_next, update

    in_specs = (P("row", "col"), P("row", "col"), P("col", None))
    out_specs = (P("row", "col"), P("col", None), P("row", "col"))
    return jax.shard_map(
        on_device, mesh=mesh, in_specs=in_specs, out_specs=out_specs, check_vma=False
    )
```

```python
import functools
import jax
import jax.numpy as jnp
from jax import lax
from jax.experimental import pallas as pl
from jax.experimental.pallas import tpu as pltpu
from jax.sharding import PartitionSpec as P

HI = lax.Precision.HIGHEST
MESH = pl.DeviceIdType.MESH
F32, BF16 = jnp.float32, jnp.bfloat16
CHUNK = 128
PANEL = 32


def rcopy(src, dst, ssem, rsem, device):
    return pltpu.make_async_remote_copy(
        src_ref=src, dst_ref=dst, send_sem=ssem, recv_sem=rsem, device_id=device, device_id_type=MESH
    )


def signal(sem, device):
    pl.semaphore_signal(sem, inc=1, device_id=device, device_id_type=MESH)


def split(a):
    hi = a.astype(BF16)
    return hi, (a - hi.astype(F32)).astype(BF16)


def dot(a, b):
    return jnp.dot(a, b, preferred_element_type=F32)


def dot3(ah, al, bh, bl):
    return dot(ah, bh) + (dot(ah, bl) + dot(al, bh))


def left_sum(chips, fused, *refs):
    if fused:
        m_ref, g_ref, rp_ref, o_ref, x, rh, rl, mbuf, gbuf, sf, *refs = refs
    else:
        x, o_ref, *refs = refs
    got, acc, sums, full, s1, r1, s2, r2, s3, r3, s4, r4 = refs
    me = lax.axis_index("col")
    core, chip = lax.rem(me, 2), me // 2
    sib = {"col": me + 1 - 2 * core}
    s = acc.shape[1]

    def place(i):
        k = lax.rem(lax.rem(i, chips) + 1, chips)
        return k, lax.rem(chip + k, chips), jnp.where(i < chips, 1 - core, core)

    def fetch(i):
        _, q, c = place(i)
        rows = pl.ds(pl.multiple_of((2 * q + c) * s, s), s)
        slot = lax.rem(i, 2)
        return (
            pltpu.make_async_copy(m_ref.at[rows], mbuf.at[slot], sf.at[0, slot]),
            pltpu.make_async_copy(g_ref.at[rows], gbuf.at[slot], sf.at[1, slot]),
        )

    if fused:
        for f in fetch(0):
            f.start()
    barrier = pltpu.get_barrier_semaphore()
    signal(barrier, sib)
    for k in range(1, chips):
        signal(barrier, {"col": 2 * lax.rem(chip + k, chips) + core})
    if fused:
        hi, lo = split(rp_ref[...])
        rh[...] = hi
        rl[...] = lo
    pl.semaphore_wait(barrier, chips)

    def pair(k):
        q = lax.rem(chip + k, chips)
        return rcopy(x.at[q, 1 - core], got.at[k], s1.at[k], r1.at[k], sib)

    def scatter(k):
        q = lax.rem(chip + k, chips)
        return rcopy(acc.at[k], sums.at[k], s2.at[k], r2.at[k], {"col": 2 * q + core})

    def turn(i, carry):
        k, q, c = place(i)
        if fused:
            @pl.when(i + 1 < 2 * chips)
            def _():
                for f in fetch(i + 1):
                    f.start()

            for f in fetch(i):
                f.wait()
            slot = lax.rem(i, 2)
            depth = rh.shape[0]
            step = divisor(depth, 512)
            total = jnp.zeros((s, rh.shape[1]), F32)
            for at in range(0, depth, step):
                here = pl.ds(at, step)
                hi, lo = split(mbuf[slot, :, here] + gbuf[slot, :, here].astype(F32))
                total = total + dot3(hi, lo, rh[here, :], rl[here, :])
            x[q, c] = total

        @pl.when(i < chips)
        def _():
            pair(k).start()

        @pl.when(i >= chips)
        def _():
            pair(k).wait_recv()
            acc[k] = x[q, core] + got[k]

            @pl.when(k > 0)
            def _():
                scatter(k).start()

        return carry

    lax.fori_loop(0, 2 * chips, turn, 0)
    total = acc[0]
    for k in range(1, chips):
        scatter(k).wait_recv()
        total = total + sums[k]
    full[chip, core] = total

    def gather(k):
        q = lax.rem(chip + k, chips)
        return rcopy(full.at[chip, core], full.at[chip, core], s3.at[k], r3.at[k], {"col": 2 * q + core})

    def forward(k):
        q = lax.rem(chip - k + chips, chips)
        return rcopy(full.at[q, core], full.at[q, core], s4.at[k], r4.at[k], sib)

    for k in range(1, chips):
        gather(k).start()
    forward(0).start()
    for k in range(1, chips):
        q = lax.rem(chip - k + chips, chips)
        rcopy(full.at[q, core], full.at[q, core], s3.at[k], r3.at[k], {"col": 2 * q + core}).wait_recv()
        forward(k).start()
    for k in range(chips):
        q = lax.rem(chip - k + chips, chips)
        rcopy(full.at[q, 1 - core], full.at[q, 1 - core], s4.at[k], r4.at[k], sib).wait_recv()
    for k in range(chips):
        pair(k).wait_send()
        forward(k).wait_send()
        if k:
            scatter(k).wait_send()
            gather(k).wait_send()
    o_ref[...] = full[...]


def left_factor(momentum, gradient, right_prev, n):
    rows, ffl = momentum.shape
    rank = right_prev.shape[1]
    chips, s = n // 2, rows // n
    fused = s % 16 == 0
    dma = pltpu.SemaphoreType.DMA
    vm = pl.BlockSpec(memory_space=pltpu.VMEM)
    hbm = pl.BlockSpec(memory_space=pl.ANY)
    if fused:
        args, specs = (momentum, gradient, right_prev), [hbm, hbm, vm]
        extra = [
            pltpu.VMEM((chips, 2, s, rank), F32),
            pltpu.VMEM((ffl, rank), BF16),
            pltpu.VMEM((ffl, rank), BF16),
            pltpu.VMEM((2, s, ffl), F32),
            pltpu.VMEM((2, s, ffl), BF16),
            dma((2, 2)),
        ]
    else:
        merged = momentum + gradient.astype(F32)
        part = jnp.dot(merged, right_prev, precision=lax.Precision.HIGH, preferred_element_type=F32)
        args, specs, extra = (part.reshape(chips, 2, s, rank),), [vm], []
    out = pl.pallas_call(
        functools.partial(left_sum, chips, fused),
        out_shape=jax.ShapeDtypeStruct((chips, 2, s, rank), F32),
        in_specs=specs,
        out_specs=vm,
        scratch_shapes=extra
        + [pltpu.VMEM((chips, s, rank), F32)] * 3
        + [pltpu.VMEM((chips, 2, s, rank), F32)]
        + [dma((chips,))] * 8,
        compiler_params=pltpu.CompilerParams(
            collective_id=0, has_side_effects=True, vmem_limit_bytes=48 * 2**20
        ),
        name="left_sum",
    )(*args)
    return out.reshape(rows, rank)


def panel_step(mat, p):
    rank, wide = mat.shape
    first = p * PANEL
    rows0 = pl.ds(pl.multiple_of(first, PANEL), PANEL)
    rows = mat[rows0, :]
    pick = lax.broadcasted_iota(jnp.int32, (rank, 128), 0) == first + lax.broadcasted_iota(
        jnp.int32, (rank, 128), 1
    )
    block = jnp.dot(rows[:, :rank], pick.astype(F32), precision=HI, preferred_element_type=F32)
    sub = lax.broadcasted_iota(jnp.int32, (PANEL, 128), 0)
    lane = lax.broadcasted_iota(jnp.int32, (PANEL, 128), 1)
    block = jnp.where(lane < PANEL, block, jnp.where(lane - PANEL == sub, 1.0, 0.0))
    for k in range(PANEL):
        col = jnp.broadcast_to(block[:, k : k + 1], (PANEL, 128))
        pivot = jnp.broadcast_to(col[k : k + 1, :], (PANEL, 128))
        inv = lax.rsqrt(pivot)
        inv = inv * (1.5 - 0.5 * (pivot * inv) * inv)
        u = jnp.broadcast_to(block[k : k + 1, :], (PANEL, 128)) * inv
        factor = jnp.where(sub > k, col * inv, 0.0)
        block = jnp.where(sub == k, u, block - factor * u)
    u = jnp.dot(block[:, PANEL : 2 * PANEL], rows, precision=HI, preferred_element_type=F32)
    mat[rows0, :] = u
    drop = lax.dot_general(
        u[:, :rank], u, (((0,), (0,)), ((), ())), precision=HI, preferred_element_type=F32
    )
    below = lax.broadcasted_iota(jnp.int32, (rank, wide), 0) >= first + PANEL
    mat[...] = jnp.where(below, mat[...] - drop, mat[...])


def times_inverse(a, inverse):
    return lax.dot_general(
        a, inverse, (((1,), (1,)), ((), ())), precision=HI, preferred_element_type=F32
    )


def right_sum(
    n, cols, ff, m_ref, g_ref, left_ref,
    next_ref, nh_ref, nl_ref, rb_ref, oh_ref, ol_ref,
    x, outer_in, inner_in, mat, colsq, lh, ll, mbuf, gbuf, sf, s_in, r_outer, s_out, r_inner, s_c, r_c,
):
    me, mc = lax.axis_index("row"), lax.axis_index("col")
    half = n // 2
    low = me < half
    depth = jnp.where(low, half - 1 - me, me - half)
    inward = {"row": jnp.where(low, me + 1, me - 1)}
    has_outer = depth < half - 1
    outward = {"row": jnp.where(has_outer, jnp.where(low, me - 1, me + 1), me)}
    rows, rank = left_ref.shape
    ffl = m_ref.shape[1]
    chunks = (rank + ffl) // CHUNK
    gram_chunks, panels = rank // CHUNK, rank // PANEL
    spread = max(chunks - gram_chunks, panels)

    def fetch(w):
        here = pl.ds(pl.multiple_of(w * CHUNK, CHUNK), CHUNK)
        slot = lax.rem(w, 2)
        return (
            pltpu.make_async_copy(m_ref.at[:, here], mbuf.at[slot], sf.at[0, slot]),
            pltpu.make_async_copy(g_ref.at[:, here], gbuf.at[slot], sf.at[1, slot]),
        )

    for f in fetch(0):
        f.start()

    barrier = pltpu.get_barrier_semaphore()
    for k in range(1, cols):
        signal(barrier, {"col": lax.rem(mc + k, cols)})
    signal(barrier, inward)

    @pl.when(has_outer)
    def _():
        signal(barrier, outward)

    for b in range(0, rows, CHUNK):
        hi, lo = split(left_ref[pl.ds(b, CHUNK), :].T)
        lh[:, pl.ds(b, CHUNK)] = hi
        ll[:, pl.ds(b, CHUNK)] = lo
    gram = lax.dot_general(
        left_ref[...], left_ref[...], (((0,), (0,)), ((), ())), precision=HI, preferred_element_type=F32
    )
    for c in range(gram_chunks):
        x[c] = gram[:, c * CHUNK : (c + 1) * CHUNK]

    @pl.when(has_outer)
    def _():
        pl.semaphore_wait(barrier, cols + 1)

    @pl.when(jnp.logical_not(has_outer))
    def _():
        pl.semaphore_wait(barrier, cols)

    def to_inner(c):
        return rcopy(x.at[c], outer_in.at[c], s_in.at[c], r_outer.at[c], inward)

    def to_partner(c):
        return rcopy(x.at[c], inner_in.at[c], s_in.at[c], r_inner.at[c], inward)

    def to_outer(c):
        return rcopy(outer_in.at[c], inner_in.at[c], s_out.at[c], r_inner.at[c], outward)

    lag = 2 + 3 * depth

    def turn(t, carry):
        @pl.when((t >= gram_chunks) & (t < chunks))
        def _():
            w = t - gram_chunks

            @pl.when(w + 1 < chunks - gram_chunks)
            def _():
                for f in fetch(w + 1):
                    f.start()

            for f in fetch(w):
                f.wait()
            slot = lax.rem(w, 2)
            step = divisor(rows, 512)
            total = jnp.zeros((rank, CHUNK), F32)
            for b in range(0, rows, step):
                here = pl.ds(b, step)
                hi, lo = split(mbuf[slot, here, :] + gbuf[slot, here, :].astype(F32))
                total = total + dot3(lh[:, here], ll[:, here], hi, lo)
            x[t] = total

        @pl.when(t < chunks)
        def _():
            @pl.when(has_outer)
            def _():
                to_inner(t).wait_recv()
                x[t] = x[t] + outer_in[t]

            @pl.when(depth > 0)
            def _():
                to_inner(t).start()

            @pl.when(depth == 0)
            def _():
                to_partner(t).start()

        c = t - lag

        @pl.when((c >= 0) & (c < chunks))
        def _():
            to_partner(c).wait_recv()

            @pl.when(depth == 0)
            def _():
                outer_in[c] = x[c] + inner_in[c]

            @pl.when(depth > 0)
            def _():
                outer_in[c] = inner_in[c]

            @pl.when(has_outer)
            def _():
                to_outer(c).start()

        @pl.when(c == gram_chunks - 1)
        def _():
            for b in range(gram_chunks):
                mat[:, pl.ds(b * CHUNK, CHUNK)] = outer_in[b]
            i0 = lax.broadcasted_iota(jnp.int32, (rank, rank), 0)
            i1 = lax.broadcasted_iota(jnp.int32, (rank, rank), 1)
            mat[:, pl.ds(rank, rank)] = jnp.where(i0 == i1, 1.0, 0.0).astype(F32)

        at = jnp.maximum(c - gram_chunks, 0)
        p = at * panels // spread

        @pl.when((c >= gram_chunks) & (c < gram_chunks + spread) & ((at + 1) * panels // spread > p))
        def _():
            panel_step(mat, p)

        return carry

    turns = gram_chunks + spread + 2 + 3 * (half - 1)
    lax.fori_loop(0, turns, turn, 0)

    inverse = mat[:, pl.ds(rank, rank)]

    def blocks(count, body, carry):
        group = max(g for g in (1, 2, 4) if count % g == 0)

        def several(b, carry):
            for g in range(group):
                carry = body(b * group + g, carry)
            return carry

        return lax.fori_loop(0, count // group, several, carry)

    def to_right(b, total):
        here = pl.ds(pl.multiple_of(b * CHUNK, CHUNK), CHUNK)
        c = b + gram_chunks
        value = jnp.dot(inverse, outer_in[c], precision=HI, preferred_element_type=F32)
        inner_in[c] = value
        rb_ref[:, here] = (0.05 * value).astype(BF16)
        return total + value * value

    part = blocks(ffl // CHUNK, to_right, jnp.zeros((rank, CHUNK), F32))
    colsq[mc] = jnp.broadcast_to(jnp.sum(part.T, axis=0, keepdims=True), (8, rank))

    def share(k):
        return rcopy(
            colsq.at[mc], colsq.at[mc], s_c.at[k - 1], r_c.at[k - 1], {"col": lax.rem(mc + k, cols)}
        )

    for k in range(1, cols):
        share(k).start()

    def to_ortho(b, carry):
        here = pl.ds(pl.multiple_of(b * CHUNK, CHUNK), CHUNK)
        hi, lo = split(times_inverse(left_ref[here, :], inverse))
        oh_ref[here, :] = hi
        ol_ref[here, :] = lo
        return carry

    blocks(rows // CHUNK, to_ortho, 0)

    for k in range(1, cols):
        q = lax.rem(mc - k + cols, cols)
        rcopy(colsq.at[q], colsq.at[q], s_c.at[k - 1], r_c.at[k - 1], {"col": q}).wait_recv()
    total = colsq[0]
    for q in range(1, cols):
        total = total + colsq[q]
    scale = jnp.broadcast_to(1.0 / jnp.sqrt(total[:1] / ff + 1e-6), (CHUNK, rank)).T

    def to_next(b, carry):
        here = pl.ds(pl.multiple_of(b * CHUNK, CHUNK), CHUNK)
        value = inner_in[b + gram_chunks] * scale
        next_ref[here, :] = value.T
        hi, lo = split(value)
        nh_ref[:, here] = hi
        nl_ref[:, here] = lo
        return carry

    blocks(ffl // CHUNK, to_next, 0)

    def drain(c, carry):
        to_inner(c).wait_send()

        @pl.when(has_outer)
        def _():
            to_outer(c).wait_send()

        return carry

    lax.fori_loop(0, chunks, drain, 0)
    for k in range(1, cols):
        share(k).wait_send()


def right_factor(momentum, gradient, left, n, cols, ff):
    (rows, rank), ffl = left.shape, momentum.shape[1]
    chunks = (rank + ffl) // CHUNK
    dma = pltpu.SemaphoreType.DMA
    vm = pl.BlockSpec(memory_space=pltpu.VMEM)
    hbm = pl.BlockSpec(memory_space=pl.ANY)
    return pl.pallas_call(
        functools.partial(right_sum, n, cols, float(ff)),
        out_shape=[jax.ShapeDtypeStruct((ffl, rank), F32)]
        + [jax.ShapeDtypeStruct((rank, ffl), BF16)] * 3
        + [jax.ShapeDtypeStruct((rows, rank), BF16)] * 2,
        in_specs=[hbm, hbm, vm],
        out_specs=[vm] * 6,
        scratch_shapes=[pltpu.VMEM((chunks, rank, CHUNK), F32)] * 3
        + [
            pltpu.VMEM((rank, 2 * rank), F32),
            pltpu.VMEM((cols, 8, rank), F32),
            pltpu.VMEM((rank, rows), BF16),
            pltpu.VMEM((rank, rows), BF16),
            pltpu.VMEM((2, rows, CHUNK), F32),
            pltpu.VMEM((2, rows, CHUNK), BF16),
            dma((2, 2)),
        ]
        + [dma((chunks,))] * 4
        + [dma((cols - 1,))] * 2,
        compiler_params=pltpu.CompilerParams(
            collective_id=1, has_side_effects=True, vmem_limit_bytes=48 * 2**20
        ),
        name="right_sum",
    )(momentum, gradient, left)


def finish(factor, m_ref, g_ref, oh_ref, ol_ref, nh_ref, nl_ref, rb_ref, new_ref, up_ref):
    oh, nh = oh_ref[...], nh_ref[...]
    new_ref[...] = (m_ref[...] + g_ref[...].astype(F32)) - dot(oh, rb_ref[...])
    up = dot(
        jnp.concatenate([oh, oh, ol_ref[...]], axis=1), jnp.concatenate([nh, nl_ref[...], nh], axis=0)
    )
    up_ref[...] = (factor * up).astype(BF16)


def divisor(size, most):
    return max(t for t in range(128, most + 1, 128) if size % t == 0)


def outputs(m, g, oh, ol, nh, nl, rb, factor):
    rows, cols = m.shape
    rank = oh.shape[1]
    tm, tn = divisor(rows, 2048), divisor(cols, 256)
    tile = pl.BlockSpec((tm, tn), lambda j, i: (i, j))
    o = pl.BlockSpec((tm, rank), lambda j, i: (i, 0))
    r = pl.BlockSpec((rank, tn), lambda j, i: (0, j))
    return pl.pallas_call(
        functools.partial(finish, factor),
        grid=(cols // tn, rows // tm),
        out_shape=[jax.ShapeDtypeStruct((rows, cols), F32), jax.ShapeDtypeStruct((rows, cols), BF16)],
        in_specs=[tile, tile, o, o, r, r, r],
        out_specs=[tile, tile],
        compiler_params=pltpu.CompilerParams(vmem_limit_bytes=48 * 2**20),
        name="finish",
    )(m, g, oh, ol, nh, nl, rb)


def solution(mesh):
    n, cols = mesh.shape["row"], mesh.shape["col"]

    def on_device(momentum, gradient, right_prev):
        ff, rank = right_prev.shape[0] * cols, right_prev.shape[1]
        d = momentum.shape[0] * n
        left = left_factor(momentum, gradient, right_prev, cols)
        right_next, nh, nl, rb, oh, ol = right_factor(momentum, gradient, left, n, cols, ff)
        new_momentum, update = outputs(
            momentum, gradient, oh, ol, nh, nl, rb, (d / rank) ** 0.5
        )
        return new_momentum, right_next, update

    in_specs = (P("row", "col"), P("row", "col"), P("col", None))
    out_specs = (P("row", "col"), P("col", None), P("row", "col"))
    return jax.shard_map(
        on_device, mesh=mesh, in_specs=in_specs, out_specs=out_specs, check_vma=False
    )
```

```python
import functools
import jax
import jax.numpy as jnp
from jax import lax
from jax.experimental import pallas as pl
from jax.experimental.pallas import tpu as pltpu
from jax.sharding import PartitionSpec as P

HI = lax.Precision.HIGHEST
MESH = pl.DeviceIdType.MESH
F32, BF16 = jnp.float32, jnp.bfloat16
CHUNK = 128
PANEL = 16


def rcopy(src, dst, ssem, rsem, device):
    return pltpu.make_async_remote_copy(
        src_ref=src, dst_ref=dst, send_sem=ssem, recv_sem=rsem, device_id=device, device_id_type=MESH
    )


def signal(sem, device):
    pl.semaphore_signal(sem, inc=1, device_id=device, device_id_type=MESH)


def split(a):
    hi = a.astype(BF16)
    return hi, (a - hi.astype(F32)).astype(BF16)


def dot(a, b):
    return jnp.dot(a, b, preferred_element_type=F32)


def dot3(ah, al, bh, bl):
    return dot(ah, bh) + (dot(ah, bl) + dot(al, bh))


def left_sum(chips, fused, *refs):
    if fused:
        m_ref, g_ref, rp_ref, o_ref, x, rh, rl, mbuf, gbuf, sf, *refs = refs
    else:
        x, o_ref, *refs = refs
    got, acc, sums, full, s1, r1, s2, r2, s3, r3, s4, r4 = refs
    me = lax.axis_index("col")
    core, chip = lax.rem(me, 2), me // 2
    sib = {"col": me + 1 - 2 * core}
    s = acc.shape[1]

    def place(i):
        k = lax.rem(lax.rem(i, chips) + 1, chips)
        return k, lax.rem(chip + k, chips), jnp.where(i < chips, 1 - core, core)

    def fetch(i):
        _, q, c = place(i)
        rows = pl.ds(pl.multiple_of((2 * q + c) * s, s), s)
        slot = lax.rem(i, 2)
        return (
            pltpu.make_async_copy(m_ref.at[rows], mbuf.at[slot], sf.at[0, slot]),
            pltpu.make_async_copy(g_ref.at[rows], gbuf.at[slot], sf.at[1, slot]),
        )

    if fused:
        for f in fetch(0):
            f.start()
    barrier = pltpu.get_barrier_semaphore()
    signal(barrier, sib)
    for k in range(1, chips):
        signal(barrier, {"col": 2 * lax.rem(chip + k, chips) + core})
    if fused:
        hi, lo = split(rp_ref[...])
        rh[...] = hi
        rl[...] = lo
    pl.semaphore_wait(barrier, chips)

    def pair(k):
        q = lax.rem(chip + k, chips)
        return rcopy(x.at[q, 1 - core], got.at[k], s1.at[k], r1.at[k], sib)

    def scatter(k):
        q = lax.rem(chip + k, chips)
        return rcopy(acc.at[k], sums.at[k], s2.at[k], r2.at[k], {"col": 2 * q + core})

    def turn(i, carry):
        k, q, c = place(i)
        if fused:
            @pl.when(i + 1 < 2 * chips)
            def _():
                for f in fetch(i + 1):
                    f.start()

            for f in fetch(i):
                f.wait()
            slot = lax.rem(i, 2)
            depth = rh.shape[0]
            step = divisor(depth, 512)
            total = jnp.zeros((s, rh.shape[1]), F32)
            for at in range(0, depth, step):
                here = pl.ds(at, step)
                hi, lo = split(mbuf[slot, :, here] + gbuf[slot, :, here].astype(F32))
                total = total + dot3(hi, lo, rh[here, :], rl[here, :])
            x[q, c] = total

        @pl.when(i < chips)
        def _():
            pair(k).start()

        @pl.when(i >= chips)
        def _():
            pair(k).wait_recv()
            acc[k] = x[q, core] + got[k]

            @pl.when(k > 0)
            def _():
                scatter(k).start()

        return carry

    lax.fori_loop(0, 2 * chips, turn, 0)
    total = acc[0]
    for k in range(1, chips):
        scatter(k).wait_recv()
        total = total + sums[k]
    full[chip, core] = total

    def gather(k):
        q = lax.rem(chip + k, chips)
        return rcopy(full.at[chip, core], full.at[chip, core], s3.at[k], r3.at[k], {"col": 2 * q + core})

    def forward(k):
        q = lax.rem(chip - k + chips, chips)
        return rcopy(full.at[q, core], full.at[q, core], s4.at[k], r4.at[k], sib)

    for k in range(1, chips):
        gather(k).start()
    forward(0).start()
    for k in range(1, chips):
        q = lax.rem(chip - k + chips, chips)
        rcopy(full.at[q, core], full.at[q, core], s3.at[k], r3.at[k], {"col": 2 * q + core}).wait_recv()
        forward(k).start()
    for k in range(chips):
        q = lax.rem(chip - k + chips, chips)
        rcopy(full.at[q, 1 - core], full.at[q, 1 - core], s4.at[k], r4.at[k], sib).wait_recv()
    for k in range(chips):
        pair(k).wait_send()
        forward(k).wait_send()
        if k:
            scatter(k).wait_send()
            gather(k).wait_send()
    o_ref[...] = full[...]


def left_factor(momentum, gradient, right_prev, n):
    rows, ffl = momentum.shape
    rank = right_prev.shape[1]
    chips, s = n // 2, rows // n
    fused = s % 16 == 0
    dma = pltpu.SemaphoreType.DMA
    vm = pl.BlockSpec(memory_space=pltpu.VMEM)
    hbm = pl.BlockSpec(memory_space=pl.ANY)
    if fused:
        args, specs = (momentum, gradient, right_prev), [hbm, hbm, vm]
        extra = [
            pltpu.VMEM((chips, 2, s, rank), F32),
            pltpu.VMEM((ffl, rank), BF16),
            pltpu.VMEM((ffl, rank), BF16),
            pltpu.VMEM((2, s, ffl), F32),
            pltpu.VMEM((2, s, ffl), BF16),
            dma((2, 2)),
        ]
    else:
        merged = momentum + gradient.astype(F32)
        part = jnp.dot(merged, right_prev, precision=lax.Precision.HIGH, preferred_element_type=F32)
        args, specs, extra = (part.reshape(chips, 2, s, rank),), [vm], []
    out = pl.pallas_call(
        functools.partial(left_sum, chips, fused),
        out_shape=jax.ShapeDtypeStruct((chips, 2, s, rank), F32),
        in_specs=specs,
        out_specs=vm,
        scratch_shapes=extra
        + [pltpu.VMEM((chips, s, rank), F32)] * 3
        + [pltpu.VMEM((chips, 2, s, rank), F32)]
        + [dma((chips,))] * 8,
        compiler_params=pltpu.CompilerParams(
            collective_id=0, has_side_effects=True, vmem_limit_bytes=48 * 2**20
        ),
        name="left_sum",
    )(*args)
    return out.reshape(rows, rank)


def panel_step(mat, p):
    rank, wide = mat.shape
    first = p * PANEL
    rows0 = pl.ds(pl.multiple_of(first, PANEL), PANEL)
    rows = mat[rows0, :]
    pick = lax.broadcasted_iota(jnp.int32, (rank, 128), 0) == first + lax.broadcasted_iota(
        jnp.int32, (rank, 128), 1
    )
    block = jnp.dot(rows[:, :rank], pick.astype(F32), precision=HI, preferred_element_type=F32)
    sub = lax.broadcasted_iota(jnp.int32, (PANEL, 128), 0)
    lane = lax.broadcasted_iota(jnp.int32, (PANEL, 128), 1)
    block = jnp.where(lane < PANEL, block, jnp.where(lane - PANEL == sub, 1.0, 0.0))
    for k in range(PANEL):
        col = jnp.broadcast_to(block[:, k : k + 1], (PANEL, 128))
        pivot = jnp.broadcast_to(col[k : k + 1, :], (PANEL, 128))
        inv = lax.rsqrt(pivot)
        inv = inv * (1.5 - 0.5 * (pivot * inv) * inv)
        u = jnp.broadcast_to(block[k : k + 1, :], (PANEL, 128)) * inv
        factor = jnp.where(sub > k, col * inv, 0.0)
        block = jnp.where(sub == k, u, block - factor * u)
    u = jnp.dot(block[:, PANEL : 2 * PANEL], rows, precision=HI, preferred_element_type=F32)
    mat[rows0, :] = u
    drop = lax.dot_general(
        u[:, :rank], u, (((0,), (0,)), ((), ())), precision=HI, preferred_element_type=F32
    )
    below = lax.broadcasted_iota(jnp.int32, (rank, wide), 0) >= first + PANEL
    mat[...] = jnp.where(below, mat[...] - drop, mat[...])


def times_inverse(a, inverse):
    return lax.dot_general(
        a, inverse, (((1,), (1,)), ((), ())), precision=HI, preferred_element_type=F32
    )


def right_sum(
    n, cols, ff, m_ref, g_ref, left_ref,
    next_ref, nh_ref, nl_ref, rb_ref, oh_ref, ol_ref,
    x, outer_in, inner_in, mat, colsq, lh, ll, mbuf, gbuf, sf, s_in, r_outer, s_out, r_inner, s_c, r_c,
):
    me, mc = lax.axis_index("row"), lax.axis_index("col")
    half = n // 2
    low = me < half
    depth = jnp.where(low, half - 1 - me, me - half)
    inward = {"row": jnp.where(low, me + 1, me - 1)}
    has_outer = depth < half - 1
    outward = {"row": jnp.where(has_outer, jnp.where(low, me - 1, me + 1), me)}
    rows, rank = left_ref.shape
    ffl = m_ref.shape[1]
    chunks = (rank + ffl) // CHUNK
    gram_chunks, panels = rank // CHUNK, rank // PANEL
    spread = max(chunks - gram_chunks, panels)

    def fetch(w):
        here = pl.ds(pl.multiple_of(w * CHUNK, CHUNK), CHUNK)
        slot = lax.rem(w, 2)
        return (
            pltpu.make_async_copy(m_ref.at[:, here], mbuf.at[slot], sf.at[0, slot]),
            pltpu.make_async_copy(g_ref.at[:, here], gbuf.at[slot], sf.at[1, slot]),
        )

    for f in fetch(0):
        f.start()

    barrier = pltpu.get_barrier_semaphore()
    for k in range(1, cols):
        signal(barrier, {"col": lax.rem(mc + k, cols)})
    signal(barrier, inward)

    @pl.when(has_outer)
    def _():
        signal(barrier, outward)

    for b in range(0, rows, CHUNK):
        hi, lo = split(left_ref[pl.ds(b, CHUNK), :].T)
        lh[:, pl.ds(b, CHUNK)] = hi
        ll[:, pl.ds(b, CHUNK)] = lo
    gram = lax.dot_general(
        left_ref[...], left_ref[...], (((0,), (0,)), ((), ())), precision=HI, preferred_element_type=F32
    )
    for c in range(gram_chunks):
        x[c] = gram[:, c * CHUNK : (c + 1) * CHUNK]

    @pl.when(has_outer)
    def _():
        pl.semaphore_wait(barrier, cols + 1)

    @pl.when(jnp.logical_not(has_outer))
    def _():
        pl.semaphore_wait(barrier, cols)

    def to_inner(c):
        return rcopy(x.at[c], outer_in.at[c], s_in.at[c], r_outer.at[c], inward)

    def to_partner(c):
        return rcopy(x.at[c], inner_in.at[c], s_in.at[c], r_inner.at[c], inward)

    def to_outer(c):
        return rcopy(outer_in.at[c], inner_in.at[c], s_out.at[c], r_inner.at[c], outward)

    lag = 2 + 3 * depth

    def turn(t, carry):
        c = t - lag
        at = jnp.maximum(c - gram_chunks, 0)
        p = at * panels // spread
        product = (t >= gram_chunks) & (t < chunks)
        panel = (c >= gram_chunks) & (c < gram_chunks + spread) & ((at + 1) * panels // spread > p)

        @pl.when(product)
        def _():
            w = t - gram_chunks

            @pl.when(w + 1 < chunks - gram_chunks)
            def _():
                for f in fetch(w + 1):
                    f.start()

            for f in fetch(w):
                f.wait()

        def multiply():
            slot = lax.rem(jnp.maximum(t - gram_chunks, 0), 2)
            step = divisor(rows, 512)
            total = jnp.zeros((rank, CHUNK), F32)
            for b in range(0, rows, step):
                here = pl.ds(b, step)
                hi, lo = split(mbuf[slot, here, :] + gbuf[slot, here, :].astype(F32))
                total = total + dot3(lh[:, here], ll[:, here], hi, lo)
            x[t] = total

        @pl.when(product & panel)
        def _():
            multiply()
            panel_step(mat, p)

        @pl.when(product & jnp.logical_not(panel))
        def _():
            multiply()

        @pl.when(panel & jnp.logical_not(product))
        def _():
            panel_step(mat, p)

        @pl.when(t < chunks)
        def _():
            @pl.when(has_outer)
            def _():
                to_inner(t).wait_recv()
                x[t] = x[t] + outer_in[t]

            @pl.when(depth > 0)
            def _():
                to_inner(t).start()

            @pl.when(depth == 0)
            def _():
                to_partner(t).start()

        @pl.when((c >= 0) & (c < chunks))
        def _():
            to_partner(c).wait_recv()

            @pl.when(depth == 0)
            def _():
                outer_in[c] = x[c] + inner_in[c]

            @pl.when(depth > 0)
            def _():
                outer_in[c] = inner_in[c]

            @pl.when(has_outer)
            def _():
                to_outer(c).start()

        @pl.when(c == gram_chunks - 1)
        def _():
            for b in range(gram_chunks):
                mat[:, pl.ds(b * CHUNK, CHUNK)] = outer_in[b]
            i0 = lax.broadcasted_iota(jnp.int32, (rank, rank), 0)
            i1 = lax.broadcasted_iota(jnp.int32, (rank, rank), 1)
            mat[:, pl.ds(rank, rank)] = jnp.where(i0 == i1, 1.0, 0.0).astype(F32)

        return carry

    turns = gram_chunks + spread + 2 + 3 * (half - 1)
    lax.fori_loop(0, turns, turn, 0)

    inverse = mat[:, pl.ds(rank, rank)]

    def blocks(count, body, carry):
        group = max(g for g in (1, 2, 4) if count % g == 0)

        def several(b, carry):
            for g in range(group):
                carry = body(b * group + g, carry)
            return carry

        return lax.fori_loop(0, count // group, several, carry)

    def to_right(b, total):
        here = pl.ds(pl.multiple_of(b * CHUNK, CHUNK), CHUNK)
        c = b + gram_chunks
        value = jnp.dot(inverse, outer_in[c], precision=HI, preferred_element_type=F32)
        inner_in[c] = value
        rb_ref[:, here] = (0.05 * value).astype(BF16)
        return total + value * value

    part = blocks(ffl // CHUNK, to_right, jnp.zeros((rank, CHUNK), F32))
    colsq[mc] = jnp.broadcast_to(jnp.sum(part.T, axis=0, keepdims=True), (8, rank))

    def share(k):
        return rcopy(
            colsq.at[mc], colsq.at[mc], s_c.at[k - 1], r_c.at[k - 1], {"col": lax.rem(mc + k, cols)}
        )

    for k in range(1, cols):
        share(k).start()

    def to_ortho(b, carry):
        here = pl.ds(pl.multiple_of(b * CHUNK, CHUNK), CHUNK)
        hi, lo = split(times_inverse(left_ref[here, :], inverse))
        oh_ref[here, :] = hi
        ol_ref[here, :] = lo
        return carry

    blocks(rows // CHUNK, to_ortho, 0)

    for k in range(1, cols):
        q = lax.rem(mc - k + cols, cols)
        rcopy(colsq.at[q], colsq.at[q], s_c.at[k - 1], r_c.at[k - 1], {"col": q}).wait_recv()
    total = colsq[0]
    for q in range(1, cols):
        total = total + colsq[q]
    scale = jnp.broadcast_to(1.0 / jnp.sqrt(total[:1] / ff + 1e-6), (CHUNK, rank)).T

    def to_next(b, carry):
        here = pl.ds(pl.multiple_of(b * CHUNK, CHUNK), CHUNK)
        value = inner_in[b + gram_chunks] * scale
        next_ref[here, :] = value.T
        hi, lo = split(value)
        nh_ref[:, here] = hi
        nl_ref[:, here] = lo
        return carry

    blocks(ffl // CHUNK, to_next, 0)

    def drain(c, carry):
        to_inner(c).wait_send()

        @pl.when(has_outer)
        def _():
            to_outer(c).wait_send()

        return carry

    lax.fori_loop(0, chunks, drain, 0)
    for k in range(1, cols):
        share(k).wait_send()


def right_factor(momentum, gradient, left, n, cols, ff):
    (rows, rank), ffl = left.shape, momentum.shape[1]
    chunks = (rank + ffl) // CHUNK
    dma = pltpu.SemaphoreType.DMA
    vm = pl.BlockSpec(memory_space=pltpu.VMEM)
    hbm = pl.BlockSpec(memory_space=pl.ANY)
    return pl.pallas_call(
        functools.partial(right_sum, n, cols, float(ff)),
        out_shape=[jax.ShapeDtypeStruct((ffl, rank), F32)]
        + [jax.ShapeDtypeStruct((rank, ffl), BF16)] * 3
        + [jax.ShapeDtypeStruct((rows, rank), BF16)] * 2,
        in_specs=[hbm, hbm, vm],
        out_specs=[vm] * 6,
        scratch_shapes=[pltpu.VMEM((chunks, rank, CHUNK), F32)] * 3
        + [
            pltpu.VMEM((rank, 2 * rank), F32),
            pltpu.VMEM((cols, 8, rank), F32),
            pltpu.VMEM((rank, rows), BF16),
            pltpu.VMEM((rank, rows), BF16),
            pltpu.VMEM((2, rows, CHUNK), F32),
            pltpu.VMEM((2, rows, CHUNK), BF16),
            dma((2, 2)),
        ]
        + [dma((chunks,))] * 4
        + [dma((cols - 1,))] * 2,
        compiler_params=pltpu.CompilerParams(
            collective_id=1, has_side_effects=True, vmem_limit_bytes=48 * 2**20
        ),
        name="right_sum",
    )(momentum, gradient, left)


def finish(factor, m_ref, g_ref, oh_ref, ol_ref, nh_ref, nl_ref, rb_ref, new_ref, up_ref):
    oh, nh = oh_ref[...], nh_ref[...]
    new_ref[...] = (m_ref[...] + g_ref[...].astype(F32)) - dot(oh, rb_ref[...])
    up = dot(
        jnp.concatenate([oh, oh, ol_ref[...]], axis=1), jnp.concatenate([nh, nl_ref[...], nh], axis=0)
    )
    up_ref[...] = (factor * up).astype(BF16)


def divisor(size, most):
    return max(t for t in range(128, most + 1, 128) if size % t == 0)


def outputs(m, g, oh, ol, nh, nl, rb, factor):
    rows, cols = m.shape
    rank = oh.shape[1]
    tm, tn = divisor(rows, 2048), divisor(cols, 256)
    tile = pl.BlockSpec((tm, tn), lambda j, i: (i, j))
    o = pl.BlockSpec((tm, rank), lambda j, i: (i, 0))
    r = pl.BlockSpec((rank, tn), lambda j, i: (0, j))
    return pl.pallas_call(
        functools.partial(finish, factor),
        grid=(cols // tn, rows // tm),
        out_shape=[jax.ShapeDtypeStruct((rows, cols), F32), jax.ShapeDtypeStruct((rows, cols), BF16)],
        in_specs=[tile, tile, o, o, r, r, r],
        out_specs=[tile, tile],
        compiler_params=pltpu.CompilerParams(vmem_limit_bytes=48 * 2**20),
        name="finish",
    )(m, g, oh, ol, nh, nl, rb)


def solution(mesh):
    n, cols = mesh.shape["row"], mesh.shape["col"]

    def on_device(momentum, gradient, right_prev):
        ff, rank = right_prev.shape[0] * cols, right_prev.shape[1]
        d = momentum.shape[0] * n
        left = left_factor(momentum, gradient, right_prev, cols)
        right_next, nh, nl, rb, oh, ol = right_factor(momentum, gradient, left, n, cols, ff)
        new_momentum, update = outputs(
            momentum, gradient, oh, ol, nh, nl, rb, (d / rank) ** 0.5
        )
        return new_momentum, right_next, update

    in_specs = (P("row", "col"), P("row", "col"), P("col", None))
    out_specs = (P("row", "col"), P("col", None), P("row", "col"))
    return jax.shard_map(
        on_device, mesh=mesh, in_specs=in_specs, out_specs=out_specs, check_vma=False
    )
```
